32 devices in a mesh: groups: 2 (over x), ctx: 16 (over z, y, core).
Axes of the slice: x: 2, y: 2, z: 4, core: 2. Of those that a mesh axis runs over, the one named last changes fastest.
Arguments:
- main_queries: bfloat16 [64, 576, 4096], P(None, None, ('groups', 'ctx')), parts along dimension 2, may hold values from -48 to 48
- main_keys: bfloat16 [576, 4096], P(None, ('groups', 'ctx')), parts along dimension 1, may hold values from -6 to 6
- index_queries: bfloat16 [64, 128, 4096], P(None, None, ('groups', 'ctx')), parts along dimension 2, may hold values from -6 to 6
- index_keys: bfloat16 [128, 4096], P(None, ('groups', 'ctx')), parts along dimension 1, may hold values from -6 to 6
- head_weights: bfloat16 [64, 4096], P(None, ('groups', 'ctx')), parts along dimension 1, may hold values from -9 to 9
- block_picks: int32 [32, 4], P(('groups', 'ctx')), parts along dimension 0, may hold values from -1 to 15, as said below
Outputs:
- row_loss: float32 [4096], P(('groups', 'ctx')), parts along dimension 0
- weight_grad: float32 [64, 4096], P(None, ('groups', 'ctx')), parts along dimension 1
- key_grad: float32 [128, 4096], P(None, ('groups', 'ctx')), parts along dimension 1
The draws below stay inside these ranges and needn't reach their ends.
There are 2 independent parts, one for each index of `groups`. The reference program is written for one: setup_inputs(seed, part) draws one part's arguments, and reference() takes and returns one part's arrays. A program takes and returns all parts, laid end to end along the dimension named above; each array names one. Nothing has to cross between parts.
Inputs may be any that keep to these rules, and one draw needn't show every extreme that they name: `block_picks`: row b names the key blocks of query block b: b itself first, then block 0 where b > 0, then other blocks below b; all named blocks differ, exactly min(b + 1, 4) are named, and the remaining entries are -1.
All inputs are finite; a program needn't handle non-finite values.
Results may differ from the reference program's by a relative error of at most 0.0027.
Values may be sent and summed in bfloat16 or wider, within the bound.
A program may use at most 128 MiB of HBM per device.

```python
import jax
import jax.numpy as jnp
from jax import lax

KD = 576
HM = 64
HI = 64
DI = 128
TOK_DEV = 128
SEL_BLOCKS = 4
TOKENS = 2048
N_CTX = 16


def shared_main_keys(key):
    return jax.random.truncated_normal(jax.random.fold_in(key, 11), -6.0, 6.0, (KD, TOKENS), jnp.float32)


def shared_index_keys(key):
    return jax.random.truncated_normal(jax.random.fold_in(key, 13), -6.0, 6.0, (DI, TOKENS), jnp.float32)


def draw_main_keys(key, part):
    values = shared_main_keys(key)
    return values.astype(jnp.bfloat16)


def draw_main_queries(key, part):
    key = jax.random.fold_in(key, 2)
    key_value = jax.random.fold_in(key, 0)
    values = jax.random.truncated_normal(key_value, -6.0, 6.0, (HM, KD, TOKENS), jnp.float32)
    return values.astype(jnp.bfloat16)


def draw_index_keys(key, part):
    values = shared_index_keys(key)
    return values.astype(jnp.bfloat16)


def draw_index_queries(key, part):
    key = jax.random.fold_in(key, 4)
    key_value = jax.random.fold_in(key, 0)
    values = jax.random.truncated_normal(key_value, -6.0, 6.0, (HI, DI, TOKENS), jnp.float32)
    return values.astype(jnp.bfloat16)


def draw_head_weights(key, part):
    key = jax.random.fold_in(key, 6)
    key_value = jax.random.fold_in(key, 0)
    values = jax.random.truncated_normal(key_value, -4.0, 4.0, (HI, TOKENS), jnp.float32)
    return values.astype(jnp.bfloat16)


def draw_block_picks(key, part):
    key = jax.random.fold_in(key, 8)
    rows = jnp.arange(N_CTX, dtype=jnp.int32)[:, None]
    blocks = jnp.arange(N_CTX, dtype=jnp.int32)[None, :]
    raw = jax.random.randint(key, (N_CTX, N_CTX), 0, 65536)
    scores = raw * N_CTX + blocks
    usable = (blocks >= 1) & (blocks < rows)
    scores = jnp.where(usable, scores, 1073741824)
    order = jnp.argsort(scores, axis=1, stable=True)[:, :SEL_BLOCKS - 2].astype(jnp.int32)
    taken = jnp.take_along_axis(scores, order, axis=1)
    others = jnp.where(taken < 1073741824, order, -1)
    second = jnp.where(rows > 0, 0, -1)
    return jnp.concatenate([rows, second, others], axis=1).astype(jnp.int32)


def setup_inputs(seed: int = 0, part: int = 0) -> dict:
    keys = jax.random.split(jax.random.key(seed), 7)
    part_splits = jax.random.split(jax.random.fold_in(keys[6], part), 7)
    main_queries = draw_main_queries(jax.random.fold_in(jax.random.fold_in(keys[6], part), 71), part)
    main_keys = draw_main_keys(jax.random.fold_in(jax.random.fold_in(keys[6], part), 71), part)
    index_queries = draw_index_queries(jax.random.fold_in(jax.random.fold_in(keys[6], part), 71), part)
    index_keys = draw_index_keys(jax.random.fold_in(jax.random.fold_in(keys[6], part), 71), part)
    head_weights = draw_head_weights(jax.random.fold_in(jax.random.fold_in(keys[6], part), 71), part)
    block_picks = draw_block_picks(jax.random.fold_in(jax.random.fold_in(keys[6], part), 71), part)
    return dict(main_queries=main_queries, main_keys=main_keys, index_queries=index_queries, index_keys=index_keys, head_weights=head_weights, block_picks=block_picks)


main_scale = 0.07216878364870322
index_scale = 0.08838834764831845
masked_value = -1.0e30


def block_terms(main_q, index_q, weights, keys_main, keys_index, picks, block):
    offsets = jnp.arange(TOK_DEV, dtype=jnp.int32)
    row_pos = block * TOK_DEV + offsets
    key_pos = (picks[:, None] * TOK_DEV + offsets[None, :]).reshape(-1)
    valid = jnp.repeat(picks >= 0, TOK_DEV)
    allowed = valid[None, :] & (key_pos[None, :] <= row_pos[:, None])
    width = SEL_BLOCKS * TOK_DEV

    def head_target(summed, query):
        scores = jnp.dot(query.T, keys_main, preferred_element_type=jnp.float32) * main_scale
        scores = jnp.where(allowed, scores, masked_value)
        highest = jnp.max(scores, axis=1, keepdims=True)
        powers = jnp.exp(scores - highest)
        return summed + powers / jnp.sum(powers, axis=1, keepdims=True), None

    summed, _ = lax.scan(head_target, jnp.zeros((TOK_DEV, width), jnp.float32), main_q)
    target = summed / HM

    def head_logit(summed_logits, parts):
        query, weight = parts
        active = jnp.maximum(jnp.dot(query.T, keys_index, preferred_element_type=jnp.float32), 0.0)
        return summed_logits + weight.astype(jnp.float32)[:, None] * active, None

    raw_logits, _ = lax.scan(head_logit, jnp.zeros((TOK_DEV, width), jnp.float32), (index_q, weights))
    logits = jnp.where(allowed, raw_logits * index_scale, masked_value)
    highest = jnp.max(logits, axis=1, keepdims=True)
    shifted = logits - highest
    powers = jnp.exp(shifted)
    denom = jnp.sum(powers, axis=1, keepdims=True)
    chosen = powers / denom
    row_loss = -jnp.sum(target * (shifted - jnp.log(denom)), axis=1)
    grad = chosen - target

    def head_grads(key_total, parts):
        query, weight = parts
        before = jnp.dot(query.T, keys_index, preferred_element_type=jnp.float32)
        active = jnp.maximum(before, 0.0)
        weight_part = jnp.sum(grad * active, axis=1) * index_scale
        upstream = jnp.where(before > 0.0, grad * weight.astype(jnp.float32)[:, None], 0.0).astype(jnp.bfloat16)
        return key_total + jnp.dot(query, upstream, preferred_element_type=jnp.float32), weight_part

    key_total, weight_grad = lax.scan(head_grads, jnp.zeros((DI, width), jnp.float32), (index_q, weights))
    key_total = key_total * index_scale
    slot_grads = jnp.transpose(key_total.reshape(DI, SEL_BLOCKS, TOK_DEV), (1, 0, 2))
    slot_grads = slot_grads * (picks >= 0).astype(jnp.float32)[:, None, None]
    return row_loss, weight_grad, slot_grads


def reference(main_queries, main_keys, index_queries, index_keys, head_weights, block_picks):
    main_blocks = main_keys.reshape(KD, N_CTX, TOK_DEV)
    index_blocks = index_keys.reshape(DI, N_CTX, TOK_DEV)

    def one_block(block):
        start = (block * TOK_DEV).astype(jnp.int32)
        picks = block_picks[block]
        safe = jnp.maximum(picks, 0).astype(jnp.int32)
        keys_main = jnp.take(main_blocks, safe, axis=1).reshape(KD, SEL_BLOCKS * TOK_DEV)
        keys_index = jnp.take(index_blocks, safe, axis=1).reshape(DI, SEL_BLOCKS * TOK_DEV)
        return block_terms(
            lax.dynamic_slice_in_dim(main_queries, start, TOK_DEV, 2),
            lax.dynamic_slice_in_dim(index_queries, start, TOK_DEV, 2),
            lax.dynamic_slice_in_dim(head_weights, start, TOK_DEV, 1),
            keys_main, keys_index, picks, block)

    losses, weight_parts, slot_parts = lax.map(one_block, jnp.arange(N_CTX, dtype=jnp.int32))
    row_loss = losses.reshape(TOKENS)
    weight_grad = jnp.transpose(weight_parts, (1, 0, 2)).reshape(HI, TOKENS)
    owners = jnp.maximum(block_picks, 0).astype(jnp.int32).reshape(-1)
    summed = jax.ops.segment_sum(slot_parts.reshape(N_CTX * SEL_BLOCKS, DI, TOK_DEV), owners, num_segments=N_CTX)
    key_grad = jnp.transpose(summed, (1, 0, 2)).reshape(DI, TOKENS)
    return (row_loss, weight_grad, key_grad)
```

```python
import functools

import jax
import jax.numpy as jnp
from jax import lax
from jax.experimental import pallas as pl
from jax.experimental.pallas import tpu as pltpu
from jax.sharding import PartitionSpec as P

main_scale = 0.07216878364870322
index_scale = 0.08838834764831845
masked_value = -1e30
log2e = 1.4426950408889634


def compute_kernel(
    picks, mq, iq, hw, k0, k1, k2, k3, loss_ref, wg_ref, slot_ref, km, ki, eye, acc, raw, kt, gr, wf
):
    step = pl.program_id(0)
    steps = pl.num_programs(0)
    tok = mq.shape[2]
    latent = mq.shape[1]
    heads = mq.shape[0]
    slots = 4
    width = slots * tok

    @pl.when(step == 0)
    def _():
        rows = lax.broadcasted_iota(jnp.int32, (tok, tok), 0)
        cols = lax.broadcasted_iota(jnp.int32, (tok, tok), 1)
        diag = jnp.where(rows == cols, 1.0, 0.0).astype(jnp.bfloat16)
        eye[:, :tok] = diag
        eye[:, tok:] = diag
        for slot, key in enumerate((k0, k1, k2, k3)):
            here = pl.ds(slot * tok, tok)
            km[here, :latent] = key[0, :latent, :].T
            ki[here, :] = key[0, latent:, :].T
            if slot == 0:
                bias = jnp.where(rows > cols, masked_value, 0.0)
            else:
                bias = jnp.full((tok, tok), jnp.where(picks[0, slot] >= 0, 0.0, masked_value))
            km[here, latent:] = bias.astype(jnp.bfloat16)
        wf[...] = hw[...].astype(jnp.float32)
        acc[...] = jnp.zeros_like(acc)
        raw[...] = jnp.zeros_like(raw)

    scale2 = main_scale * log2e

    def main_pair(i, _):
        h = 2 * i
        pair = jnp.concatenate([mq[h], mq[h + 1]], axis=1)
        query = jnp.concatenate([pair, eye[...]], axis=0)
        s = jnp.dot(km[...], query, preferred_element_type=jnp.float32)
        m = jnp.max(s, axis=0, keepdims=True)
        p = jnp.exp2((s - m) * scale2)
        p = p * (1.0 / jnp.sum(p, axis=0, keepdims=True))
        acc[...] += p[:, :tok] + p[:, tok:]
        j = step * heads + h
        ipair = jnp.concatenate([iq[j], iq[j + 1]], axis=1)
        before = jnp.dot(ki[...], ipair, preferred_element_type=jnp.float32)
        w = jnp.concatenate(
            [wf[pl.ds(j, 1), :], wf[pl.ds(j + 1, 1), :]], axis=1
        )
        a = jnp.maximum(before, 0.0) * w
        raw[...] += a[:, :tok] + a[:, tok:]
        return 0

    lax.fori_loop(0, heads // 2, main_pair, 0, unroll=2)

    @pl.when(step == steps - 1)
    def _():
        total_heads = heads * steps
        index_heads = iq.shape[0]
        target = acc[...] * (1.0 / total_heads)
        bias = km[:, latent:].astype(jnp.float32)
        logits = jnp.where(bias < 0.0, masked_value, raw[...] * index_scale)
        highest = jnp.max(logits, axis=0, keepdims=True)
        shifted = logits - highest
        powers = jnp.exp(shifted)
        denom = jnp.sum(powers, axis=0, keepdims=True)
        loss_ref[...] = -jnp.sum(target * (shifted - jnp.log(denom)), axis=0, keepdims=True)
        grad = powers / denom - target
        gr[:, :tok] = grad
        gr[:, tok:] = grad
        kt[...] = jnp.zeros_like(kt)

        def back_pair(i, _):
            j = 2 * i
            ipair = jnp.concatenate([iq[j], iq[j + 1]], axis=1)
            before = jnp.dot(ki[...], ipair, preferred_element_type=jnp.float32)
            g = gr[...]
            w = jnp.concatenate(
                [wf[pl.ds(j, 1), :], wf[pl.ds(j + 1, 1), :]], axis=1
            )
            part = jnp.sum(g * jnp.maximum(before, 0.0), axis=0, keepdims=True) * index_scale
            wg_ref[pl.ds(j, 1), :] = part[:, :tok]
            wg_ref[pl.ds(j + 1, 1), :] = part[:, tok:]
            up = jnp.where(before > 0.0, g * w, 0.0).astype(jnp.bfloat16)
            kt[...] += lax.dot_general(
                up, ipair, (((1,), (1,)), ((), ())), preferred_element_type=jnp.float32
            )
            return 0

        lax.fori_loop(0, index_heads // 2, back_pair, 0, unroll=2)
        for slot in range(slots):
            slot_ref[slot] = (kt[pl.ds(slot * tok, tok), :] * index_scale).T


def compute(picks, mq, iq, hw, keys):
    heads, latent, tok = mq.shape
    index_heads, dim, _ = iq.shape
    channels = latent + dim
    group = 8
    width = 4 * tok

    def key_spec(slot):
        return pl.BlockSpec(
            (1, channels, tok), lambda g, p: (jnp.maximum(p[0, slot], 0), 0, 0)
        )

    spec = pltpu.PrefetchScalarGridSpec(
        num_scalar_prefetch=1,
        grid=(heads // group,),
        in_specs=[
            pl.BlockSpec((group, latent, tok), lambda g, p: (g, 0, 0)),
            pl.BlockSpec((index_heads, dim, tok), lambda g, p: (0, 0, 0)),
            pl.BlockSpec((index_heads, tok), lambda g, p: (0, 0)),
        ]
        + [key_spec(slot) for slot in range(4)],
        out_specs=[
            pl.BlockSpec((1, tok), lambda g, p: (0, 0)),
            pl.BlockSpec((index_heads, tok), lambda g, p: (0, 0)),
            pl.BlockSpec((4, dim, tok), lambda g, p: (0, 0, 0)),
        ],
        scratch_shapes=[
            pltpu.VMEM((width, latent + tok), jnp.bfloat16),
            pltpu.VMEM((width, dim), jnp.bfloat16),
            pltpu.VMEM((tok, 2 * tok), jnp.bfloat16),
            pltpu.VMEM((width, tok), jnp.float32),
            pltpu.VMEM((width, tok), jnp.float32),
            pltpu.VMEM((width, dim), jnp.float32),
            pltpu.VMEM((width, 2 * tok), jnp.float32),
            pltpu.VMEM((index_heads, tok), jnp.float32),
        ],
    )
    return pl.pallas_call(
        compute_kernel,
        grid_spec=spec,
        out_shape=[
            jax.ShapeDtypeStruct((1, tok), jnp.float32),
            jax.ShapeDtypeStruct((index_heads, tok), jnp.float32),
            jax.ShapeDtypeStruct((4, dim, tok), jnp.float32),
        ],
        compiler_params=pltpu.CompilerParams(vmem_limit_bytes=48 * 1024 * 1024),
    )(picks, mq, iq, hw, keys, keys, keys, keys)


def shards(main_queries, main_keys, index_queries, index_keys, head_weights, block_picks):
    tok = main_queries.shape[2]
    picks = block_picks
    count = lax.axis_size("ctx")
    packed = jnp.concatenate([main_keys, index_keys], axis=0)
    keys = lax.all_gather(packed, "ctx", axis=0, tiled=False)
    row_loss, weight_grad, slot_grads = compute(
        picks, main_queries, index_queries, head_weights, keys
    )
    owners = jnp.arange(count, dtype=jnp.int32)
    match = picks[0][:, None] == owners[None, :]
    outgoing = jnp.zeros((count,) + slot_grads.shape[1:], jnp.float32)
    for slot in range(4):
        outgoing = outgoing + jnp.where(match[slot][:, None, None], slot_grads[slot][None], 0.0)
    arrived = lax.all_to_all(outgoing, "ctx", split_axis=0, concat_axis=0, tiled=True)
    key_grad = jnp.sum(arrived, axis=0)
    return (row_loss.reshape(tok), weight_grad, key_grad)


def solution(mesh):
    in_specs = (
        P(None, None, ("groups", "ctx")),
        P(None, ("groups", "ctx")),
        P(None, None, ("groups", "ctx")),
        P(None, ("groups", "ctx")),
        P(None, ("groups", "ctx")),
        P(("groups", "ctx"), None),
    )
    out_specs = (P(("groups", "ctx")), P(None, ("groups", "ctx")), P(None, ("groups", "ctx")))
    return jax.shard_map(shards, mesh=mesh, in_specs=in_specs, out_specs=out_specs, check_vma=False)
```

```python
import functools

import jax
import jax.numpy as jnp
from jax import lax
from jax.experimental import pallas as pl
from jax.experimental.pallas import tpu as pltpu
from jax.sharding import PartitionSpec as P

main_scale = 0.07216878364870322
index_scale = 0.08838834764831845
masked_value = -1e30
log2e = 1.4426950408889634


def compute_kernel(
    picks, mq, iq, hw, k0, k1, k2, k3, loss_ref, wg_ref, slot_ref, km, ki, eye, acc, raw, kt, gr, wf
):
    step = pl.program_id(0)
    steps = pl.num_programs(0)
    tok = mq.shape[2]
    latent = mq.shape[1]
    heads = mq.shape[0]
    slots = 4
    width = slots * tok

    @pl.when(step == 0)
    def _():
        rows = lax.broadcasted_iota(jnp.int32, (tok, tok), 0)
        cols = lax.broadcasted_iota(jnp.int32, (tok, tok), 1)
        diag = jnp.where(rows == cols, 1.0, 0.0).astype(jnp.bfloat16)
        eye[:, :tok] = diag
        eye[:, tok:] = diag
        for slot, key in enumerate((k0, k1, k2, k3)):
            here = pl.ds(slot * tok, tok)
            km[here, :latent] = key[0, :latent, :].T
            ki[here, :] = key[0, latent:, :].T
            if slot == 0:
                bias = jnp.where(rows > cols, masked_value, 0.0)
            else:
                bias = jnp.full((tok, tok), jnp.where(picks[0, slot] >= 0, 0.0, masked_value))
            km[here, latent:] = bias.astype(jnp.bfloat16)
        wf[...] = hw[...].astype(jnp.float32)
        acc[...] = jnp.zeros_like(acc)
        raw[...] = jnp.zeros_like(raw)

    scale2 = main_scale * log2e

    def main_pair(i, _):
        h = 2 * i
        pair = jnp.concatenate([mq[h], mq[h + 1]], axis=1)
        query = jnp.concatenate([pair, eye[...]], axis=0)
        s = jnp.dot(km[...], query, preferred_element_type=jnp.float32)
        m = jnp.max(s, axis=0, keepdims=True)
        p = jnp.exp2((s - m) * scale2)
        p = p * (1.0 / jnp.sum(p, axis=0, keepdims=True))
        acc[...] += p[:, :tok] + p[:, tok:]
        j = step * heads + h
        ipair = jnp.concatenate([iq[j], iq[j + 1]], axis=1)
        before = jnp.dot(ki[...], ipair, preferred_element_type=jnp.float32)
        w = jnp.concatenate(
            [wf[pl.ds(j, 1), :], wf[pl.ds(j + 1, 1), :]], axis=1
        )
        a = jnp.maximum(before, 0.0) * w
        raw[...] += a[:, :tok] + a[:, tok:]
        return 0

    lax.fori_loop(0, heads // 2, main_pair, 0, unroll=2)

    @pl.when(step == steps - 1)
    def _():
        total_heads = heads * steps
        index_heads = iq.shape[0]
        target = acc[...] * (1.0 / total_heads)
        bias = km[:, latent:].astype(jnp.float32)
        logits = jnp.where(bias < 0.0, masked_value, raw[...] * index_scale)
        highest = jnp.max(logits, axis=0, keepdims=True)
        shifted = logits - highest
        powers = jnp.exp(shifted)
        denom = jnp.sum(powers, axis=0, keepdims=True)
        loss_ref[...] = -jnp.sum(target * (shifted - jnp.log(denom)), axis=0, keepdims=True)
        grad = powers / denom - target
        gr[:, :tok] = grad
        gr[:, tok:] = grad
        kt[...] = jnp.zeros_like(kt)

        def back_pair(i, _):
            j = 2 * i
            ipair = jnp.concatenate([iq[j], iq[j + 1]], axis=1)
            before = jnp.dot(ki[...], ipair, preferred_element_type=jnp.float32)
            g = gr[...]
            w = jnp.concatenate(
                [wf[pl.ds(j, 1), :], wf[pl.ds(j + 1, 1), :]], axis=1
            )
            part = jnp.sum(g * jnp.maximum(before, 0.0), axis=0, keepdims=True) * index_scale
            wg_ref[pl.ds(j, 1), :] = part[:, :tok]
            wg_ref[pl.ds(j + 1, 1), :] = part[:, tok:]
            up = jnp.where(before > 0.0, g * w, 0.0).astype(jnp.bfloat16)
            kt[...] += lax.dot_general(
                up, ipair, (((1,), (1,)), ((), ())), preferred_element_type=jnp.float32
            )
            return 0

        lax.fori_loop(0, index_heads // 2, back_pair, 0, unroll=2)
        for slot in range(slots):
            slot_ref[slot] = (kt[pl.ds(slot * tok, tok), :] * index_scale).T


def compute(picks, mq, iq, hw, keys):
    heads, latent, tok = mq.shape
    index_heads, dim, _ = iq.shape
    channels = latent + dim
    group = 8
    width = 4 * tok

    def key_spec(slot):
        return pl.BlockSpec(
            (1, channels, tok), lambda g, p: (jnp.maximum(p[0, slot], 0), 0, 0)
        )

    spec = pltpu.PrefetchScalarGridSpec(
        num_scalar_prefetch=1,
        grid=(heads // group,),
        in_specs=[
            pl.BlockSpec((group, latent, tok), lambda g, p: (g, 0, 0)),
            pl.BlockSpec((index_heads, dim, tok), lambda g, p: (0, 0, 0)),
            pl.BlockSpec((index_heads, tok), lambda g, p: (0, 0)),
        ]
        + [key_spec(slot) for slot in range(4)],
        out_specs=[
            pl.BlockSpec((1, tok), lambda g, p: (0, 0)),
            pl.BlockSpec((index_heads, tok), lambda g, p: (0, 0)),
            pl.BlockSpec((4, dim, tok), lambda g, p: (0, 0, 0)),
        ],
        scratch_shapes=[
            pltpu.VMEM((width, latent + tok), jnp.bfloat16),
            pltpu.VMEM((width, dim), jnp.bfloat16),
            pltpu.VMEM((tok, 2 * tok), jnp.bfloat16),
            pltpu.VMEM((width, tok), jnp.float32),
            pltpu.VMEM((width, tok), jnp.float32),
            pltpu.VMEM((width, dim), jnp.float32),
            pltpu.VMEM((width, 2 * tok), jnp.float32),
            pltpu.VMEM((index_heads, tok), jnp.float32),
        ],
    )
    return pl.pallas_call(
        compute_kernel,
        grid_spec=spec,
        out_shape=[
            jax.ShapeDtypeStruct((1, tok), jnp.float32),
            jax.ShapeDtypeStruct((index_heads, tok), jnp.float32),
            jax.ShapeDtypeStruct((4, dim, tok), jnp.float32),
        ],
        compiler_params=pltpu.CompilerParams(vmem_limit_bytes=48 * 1024 * 1024),
    )(picks, mq, iq, hw, keys, keys, keys, keys)


mesh_ids = pl.DeviceIdType.MESH


def layout(count):
    half = count // 2
    mid = 1
    while 4 * mid * mid <= half:
        mid *= 2
    return half // mid, mid


def position(mid):
    me = lax.axis_index("ctx")
    return me // (2 * mid), lax.rem(me // 2, mid), lax.rem(me, 2)


def greet(peers):
    barrier = pltpu.get_barrier_semaphore()
    for peer in peers:
        pl.semaphore_signal(barrier, inc=1, device_id={"ctx": peer}, device_id_type=mesh_ids)
    pl.semaphore_wait(barrier, len(peers))


def gather_kernel(count, main_ref, index_ref, out, local_sem, recv, zsend, ysend, csend):
    outer, mid = layout(count)
    a, y, c = position(mid)
    latent = main_ref.shape[0]
    channels = latent + index_ref.shape[0]

    def name(level, row, core):
        return (level * mid + row) * 2 + core

    me = name(a, y, c)
    own = [
        pltpu.make_async_copy(main_ref, out.at[me, pl.ds(0, latent)], local_sem.at[0]),
        pltpu.make_async_copy(
            index_ref, out.at[me, pl.ds(latent, channels - latent)], local_sem.at[1]
        ),
    ]
    for copy in own:
        copy.start()
    greet(
        [name(lax.rem(a + d, outer), y, c) for d in range(1, outer)]
        + [name(a, lax.rem(y + d, mid), c) for d in range(1, mid)]
        + [name(a, y, 1 - c)]
    )
    for copy in own:
        copy.wait()

    def send(block, peer, sem):
        return pltpu.make_async_remote_copy(
            src_ref=out.at[block],
            dst_ref=out.at[block],
            send_sem=sem,
            recv_sem=recv.at[block],
            device_id={"ctx": peer},
            device_id_type=mesh_ids,
        )

    def up(k):
        return send(name(a - k, y, c), name(a + 1, y, c), zsend.at[k])

    def side(k, d):
        return send(
            name(a - k, y, c), name(a, lax.rem(y + d, mid), c), ysend.at[k * max(mid - 1, 1) + d - 1]
        )

    def across(k, d):
        return send(
            name(a - k, lax.rem(y + d, mid), c), name(a, y, 1 - c), csend.at[k * mid + d]
        )

    def arrive(block):
        send(block, name(a, y, 1 - c), csend.at[0]).wait_recv()

    def first(k):
        @pl.when(a >= k)
        def _():
            if k > 0:
                arrive(name(a - k, y, c))

            @pl.when(a + 1 < outer)
            def _():
                up(k).start()

            for d in range(1, mid):
                side(k, d).start()
            across(k, 0).start()

    def second(k):
        @pl.when(a >= k)
        def _():
            for d in range(1, mid):
                arrive(name(a - k, lax.rem(y + d, mid), c))
                across(k, d).start()

    for k in range(outer):
        first(k)
        if k > 0:
            second(k - 1)
    second(outer - 1)
    for k in range(outer):

        @pl.when(a >= k)
        def _():
            for d in range(mid):
                arrive(name(a - k, lax.rem(y + d, mid), 1 - c))

            @pl.when(a + 1 < outer)
            def _():
                up(k).wait_send()

            for d in range(1, mid):
                side(k, d).wait_send()
            for d in range(mid):
                across(k, d).wait_send()


def gather(main_keys, index_keys):
    count = lax.axis_size("ctx")
    outer, mid = layout(count)
    channels = main_keys.shape[0] + index_keys.shape[0]
    return pl.pallas_call(
        functools.partial(gather_kernel, count),
        out_shape=jax.ShapeDtypeStruct((count, channels, main_keys.shape[1]), jnp.bfloat16),
        in_specs=[pl.BlockSpec(memory_space=pl.ANY)] * 2,
        out_specs=pl.BlockSpec(memory_space=pl.ANY),
        scratch_shapes=[
            pltpu.SemaphoreType.DMA((2,)),
            pltpu.SemaphoreType.DMA((count,)),
            pltpu.SemaphoreType.DMA((outer,)),
            pltpu.SemaphoreType.DMA((outer * max(mid - 1, 1),)),
            pltpu.SemaphoreType.DMA((outer * mid,)),
        ],
        compiler_params=pltpu.CompilerParams(collective_id=0, has_side_effects=True),
    )(main_keys, index_keys)


def scatter_kernel(count, terms, out, buf1, sum1, buf2, sum2, buf3, s1, r1, s2, r2, s3, r3):
    outer, mid = layout(count)
    a, y, c = position(mid)
    others = max(mid - 1, 1)

    def name(level, row, core):
        return (level * mid + row) * 2 + core

    greet(
        [name(lax.rem(a + d, outer), y, c) for d in range(1, outer)]
        + [name(a, lax.rem(y + d, mid), c) for d in range(1, mid)]
        + [name(a, y, 1 - c)]
    )

    def send(src, dst, send_sem, recv_sem, peer):
        return pltpu.make_async_remote_copy(
            src_ref=src,
            dst_ref=dst,
            send_sem=send_sem,
            recv_sem=recv_sem,
            device_id={"ctx": peer},
            device_id_type=mesh_ids,
        )

    def across(k):
        return send(terms.at[1 - c, k], buf1.at[k], s1.at[k], r1.at[k], name(a, y, 1 - c))

    def side(k, d):
        row = lax.rem(y + d, mid)
        spot = k * others + d - 1
        return send(sum1.at[k, row], buf2.at[spot], s2.at[spot], r2.at[spot], name(a, row, c))

    def down(k):
        spot = a - k - 1
        return send(sum2.at[k], buf3.at[spot], s3.at[k], r3.at[spot], name(k, y, c))

    for k in range(outer):

        @pl.when(a >= k)
        def _():
            across(k).start()

    for k in range(outer):

        @pl.when(a >= k)
        def _():
            across(k).wait_recv()
            sum1[k] = terms[c, k] + buf1[k]
            for d in range(1, mid):
                side(k, d).start()

    for k in range(outer):

        @pl.when(a >= k)
        def _():
            total = sum1[k, y]
            for d in range(1, mid):
                side(k, d).wait_recv()
                total = total + buf2[k * others + d - 1]
            sum2[k] = total

            @pl.when(a > k)
            def _():
                down(k).start()

            @pl.when(a == k)
            def _():
                out[...] = total

    for d in range(outer - 1):

        @pl.when(a + d + 1 < outer)
        def _():
            send(sum2.at[0], buf3.at[d], s3.at[0], r3.at[d], name(a, y, 1 - c)).wait_recv()
            out[...] += buf3[d]

    for k in range(outer):

        @pl.when(a >= k)
        def _():
            across(k).wait_send()
            for d in range(1, mid):
                side(k, d).wait_send()

            @pl.when(a > k)
            def _():
                down(k).wait_send()


def scatter(terms):
    count = lax.axis_size("ctx")
    outer, mid = layout(count)
    others = max(mid - 1, 1)
    tile = terms.shape[3:]
    return pl.pallas_call(
        functools.partial(scatter_kernel, count),
        out_shape=jax.ShapeDtypeStruct(tile, jnp.float32),
        in_specs=[pl.BlockSpec(memory_space=pltpu.VMEM)],
        out_specs=pl.BlockSpec(memory_space=pltpu.VMEM),
        scratch_shapes=[
            pltpu.VMEM((outer, mid) + tile, jnp.float32),
            pltpu.VMEM((outer, mid) + tile, jnp.float32),
            pltpu.VMEM((outer * others,) + tile, jnp.float32),
            pltpu.VMEM((outer,) + tile, jnp.float32),
            pltpu.VMEM((outer - 1,) + tile, jnp.float32),
            pltpu.SemaphoreType.DMA((outer,)),
            pltpu.SemaphoreType.DMA((outer,)),
            pltpu.SemaphoreType.DMA((outer * others,)),
            pltpu.SemaphoreType.DMA((outer * others,)),
            pltpu.SemaphoreType.DMA((outer,)),
            pltpu.SemaphoreType.DMA((outer - 1,)),
        ],
        compiler_params=pltpu.CompilerParams(
            collective_id=1, has_side_effects=True, vmem_limit_bytes=48 * 1024 * 1024
        ),
    )(terms)


def shards(main_queries, main_keys, index_queries, index_keys, head_weights, block_picks):
    tok = main_queries.shape[2]
    picks = block_picks
    count = lax.axis_size("ctx")
    keys = gather(main_keys, index_keys)
    row_loss, weight_grad, slot_grads = compute(
        picks, main_queries, index_queries, head_weights, keys
    )
    outer, mid = layout(count)
    owners = jnp.arange(count, dtype=jnp.int32).reshape(outer, mid, 2).transpose(2, 0, 1)
    terms = jnp.zeros(owners.shape + slot_grads.shape[1:], jnp.float32)
    for slot in range(4):
        match = (picks[0, slot] == owners)[..., None, None]
        terms = terms + jnp.where(match, slot_grads[slot], 0.0)
    key_grad = scatter(terms)
    return (row_loss.reshape(tok), weight_grad, key_grad)


def solution(mesh):
    in_specs = (
        P(None, None, ("groups", "ctx")),
        P(None, ("groups", "ctx")),
        P(None, None, ("groups", "ctx")),
        P(None, ("groups", "ctx")),
        P(None, ("groups", "ctx")),
        P(("groups", "ctx"), None),
    )
    out_specs = (P(("groups", "ctx")), P(None, ("groups", "ctx")), P(None, ("groups", "ctx")))
    return jax.shard_map(shards, mesh=mesh, in_specs=in_specs, out_specs=out_specs, check_vma=False)
```

```python
import functools

import jax
import jax.numpy as jnp
from jax import lax
from jax.experimental import pallas as pl
from jax.experimental.pallas import tpu as pltpu
from jax.sharding import PartitionSpec as P

main_scale = 0.07216878364870322
index_scale = 0.08838834764831845
masked_value = -1e30
log2e = 1.4426950408889634


def compute_kernel(
    picks, mq, iq, hw, k0, k1, k2, k3, loss_ref, wg_ref, slot_ref, km, ki, eye, acc, raw, kt, gr, wf
):
    step = pl.program_id(0)
    steps = pl.num_programs(0)
    tok = mq.shape[2]
    latent = mq.shape[1]
    heads = mq.shape[0]
    slots = 4
    width = slots * tok

    @pl.when(step == 0)
    def _():
        rows = lax.broadcasted_iota(jnp.int32, (tok, tok), 0)
        cols = lax.broadcasted_iota(jnp.int32, (tok, tok), 1)
        diag = jnp.where(rows == cols, 1.0, 0.0).astype(jnp.bfloat16)
        eye[:, :tok] = diag
        eye[:, tok:] = diag
        for slot, key in enumerate((k0, k1, k2, k3)):
            here = pl.ds(slot * tok, tok)
            km[here, :latent] = key[0, :latent, :].T
            ki[here, :] = key[0, latent:, :].T
            if slot == 0:
                bias = jnp.where(rows > cols, masked_value, 0.0)
            else:
                bias = jnp.full((tok, tok), jnp.where(picks[0, slot] >= 0, 0.0, masked_value))
            km[here, latent:] = bias.astype(jnp.bfloat16)
        wf[...] = hw[...].astype(jnp.float32)
        acc[...] = jnp.zeros_like(acc)
        raw[...] = jnp.zeros_like(raw)
        slot_ref[...] = jnp.zeros_like(slot_ref)

    scale2 = main_scale * log2e

    def main_pair(i, _):
        h = 2 * i
        pair = jnp.concatenate([mq[h], mq[h + 1]], axis=1)
        query = jnp.concatenate([pair, eye[...]], axis=0)
        s = jnp.dot(km[...], query, preferred_element_type=jnp.float32)
        m = jnp.max(s, axis=0, keepdims=True)
        p = jnp.exp2((s - m) * scale2)
        p = p * (1.0 / jnp.sum(p, axis=0, keepdims=True))
        acc[...] += p[:, :tok] + p[:, tok:]
        j = step * heads + h
        ipair = jnp.concatenate([iq[j], iq[j + 1]], axis=1)
        before = jnp.dot(ki[...], ipair, preferred_element_type=jnp.float32)
        w = jnp.concatenate(
            [wf[pl.ds(j, 1), :], wf[pl.ds(j + 1, 1), :]], axis=1
        )
        a = jnp.maximum(before, 0.0) * w
        raw[...] += a[:, :tok] + a[:, tok:]
        return 0

    lax.fori_loop(0, heads // 2, main_pair, 0, unroll=2)

    @pl.when(step == steps - 1)
    def _():
        total_heads = heads * steps
        index_heads = iq.shape[0]
        target = acc[...] * (1.0 / total_heads)
        bias = km[:, latent:].astype(jnp.float32)
        logits = jnp.where(bias < 0.0, masked_value, raw[...] * index_scale)
        highest = jnp.max(logits, axis=0, keepdims=True)
        shifted = logits - highest
        powers = jnp.exp(shifted)
        denom = jnp.sum(powers, axis=0, keepdims=True)
        loss_ref[...] = -jnp.sum(target * (shifted - jnp.log(denom)), axis=0, keepdims=True)
        grad = powers / denom - target
        gr[:, :tok] = grad
        gr[:, tok:] = grad
        kt[...] = jnp.zeros_like(kt)

        def back_pair(i, _):
            j = 2 * i
            ipair = jnp.concatenate([iq[j], iq[j + 1]], axis=1)
            before = jnp.dot(ki[...], ipair, preferred_element_type=jnp.float32)
            g = gr[...]
            w = jnp.concatenate(
                [wf[pl.ds(j, 1), :], wf[pl.ds(j + 1, 1), :]], axis=1
            )
            part = jnp.sum(g * jnp.maximum(before, 0.0), axis=0, keepdims=True) * index_scale
            wg_ref[pl.ds(j, 1), :] = part[:, :tok]
            wg_ref[pl.ds(j + 1, 1), :] = part[:, tok:]
            up = jnp.where(before > 0.0, g * w, 0.0).astype(jnp.bfloat16)
            kt[...] += lax.dot_general(
                up, ipair, (((1,), (1,)), ((), ())), preferred_element_type=jnp.float32
            )
            return 0

        lax.fori_loop(0, index_heads // 2, back_pair, 0, unroll=2)
        for slot in range(slots):
            part = (kt[pl.ds(slot * tok, tok), :] * index_scale).T
            owner = picks[0, slot]
            half = slot_ref.shape[0] // 2

            @pl.when(owner >= 0)
            def _():
                slot_ref[lax.rem(owner, 2) * half + owner // 2] = part


def compute(picks, mq, iq, hw, keys):
    heads, latent, tok = mq.shape
    index_heads, dim, _ = iq.shape
    channels = latent + dim
    group = 8
    count = keys.shape[0]
    width = 4 * tok

    def key_spec(slot):
        return pl.BlockSpec(
            (1, channels, tok), lambda g, p: (jnp.maximum(p[0, slot], 0), 0, 0)
        )

    spec = pltpu.PrefetchScalarGridSpec(
        num_scalar_prefetch=1,
        grid=(heads // group,),
        in_specs=[
            pl.BlockSpec((group, latent, tok), lambda g, p: (g, 0, 0)),
            pl.BlockSpec((index_heads, dim, tok), lambda g, p: (0, 0, 0)),
            pl.BlockSpec((index_heads, tok), lambda g, p: (0, 0)),
        ]
        + [key_spec(slot) for slot in range(4)],
        out_specs=[
            pl.BlockSpec((1, tok), lambda g, p: (0, 0)),
            pl.BlockSpec((index_heads, tok), lambda g, p: (0, 0)),
            pl.BlockSpec((count, dim, tok), lambda g, p: (0, 0, 0)),
        ],
        scratch_shapes=[
            pltpu.VMEM((width, latent + tok), jnp.bfloat16),
            pltpu.VMEM((width, dim), jnp.bfloat16),
            pltpu.VMEM((tok, 2 * tok), jnp.bfloat16),
            pltpu.VMEM((width, tok), jnp.float32),
            pltpu.VMEM((width, tok), jnp.float32),
            pltpu.VMEM((width, dim), jnp.float32),
            pltpu.VMEM((width, 2 * tok), jnp.float32),
            pltpu.VMEM((index_heads, tok), jnp.float32),
        ],
    )
    return pl.pallas_call(
        compute_kernel,
        grid_spec=spec,
        out_shape=[
            jax.ShapeDtypeStruct((1, tok), jnp.float32),
            jax.ShapeDtypeStruct((index_heads, tok), jnp.float32),
            jax.ShapeDtypeStruct((count, dim, tok), jnp.float32),
        ],
        compiler_params=pltpu.CompilerParams(vmem_limit_bytes=48 * 1024 * 1024),
    )(picks, mq, iq, hw, keys, keys, keys, keys)


mesh_ids = pl.DeviceIdType.MESH


def layout(count):
    half = count // 2
    mid = 1
    while 4 * mid * mid <= half:
        mid *= 2
    return half // mid, mid


def position(mid):
    me = lax.axis_index("ctx")
    return me // (2 * mid), lax.rem(me // 2, mid), lax.rem(me, 2)


def greet(peers):
    barrier = pltpu.get_barrier_semaphore()
    for peer in peers:
        pl.semaphore_signal(barrier, inc=1, device_id={"ctx": peer}, device_id_type=mesh_ids)
    pl.semaphore_wait(barrier, len(peers))


def gather_kernel(count, main_ref, index_ref, out, local_sem, recv, zsend, ysend, csend):
    outer, mid = layout(count)
    a, y, c = position(mid)
    latent = main_ref.shape[0]
    channels = latent + index_ref.shape[0]

    def name(level, row, core):
        return (level * mid + row) * 2 + core

    me = name(a, y, c)
    own = [
        pltpu.make_async_copy(main_ref, out.at[me, pl.ds(0, latent)], local_sem.at[0]),
        pltpu.make_async_copy(
            index_ref, out.at[me, pl.ds(latent, channels - latent)], local_sem.at[1]
        ),
    ]
    for copy in own:
        copy.start()
    greet(
        [name(lax.rem(a + d, outer), y, c) for d in range(1, outer)]
        + [name(a, lax.rem(y + d, mid), c) for d in range(1, mid)]
        + [name(a, y, 1 - c)]
    )
    for copy in own:
        copy.wait()

    def send(block, peer, sem):
        return pltpu.make_async_remote_copy(
            src_ref=out.at[block],
            dst_ref=out.at[block],
            send_sem=sem,
            recv_sem=recv.at[block],
            device_id={"ctx": peer},
            device_id_type=mesh_ids,
        )

    def up(k):
        return send(name(a - k, y, c), name(a + 1, y, c), zsend.at[k])

    def side(k, d):
        return send(
            name(a - k, y, c), name(a, lax.rem(y + d, mid), c), ysend.at[k * max(mid - 1, 1) + d - 1]
        )

    def across(k, d):
        return send(
            name(a - k, lax.rem(y + d, mid), c), name(a, y, 1 - c), csend.at[k * mid + d]
        )

    def arrive(block):
        send(block, name(a, y, 1 - c), csend.at[0]).wait_recv()

    def first(k):
        @pl.when(a >= k)
        def _():
            if k > 0:
                arrive(name(a - k, y, c))

            @pl.when(a + 1 < outer)
            def _():
                up(k).start()

            for d in range(1, mid):
                side(k, d).start()
            across(k, 0).start()

    def second(k):
        @pl.when(a >= k)
        def _():
            for d in range(1, mid):
                arrive(name(a - k, lax.rem(y + d, mid), c))
                across(k, d).start()

    for k in range(outer):
        first(k)
        if k > 0:
            second(k - 1)
    second(outer - 1)
    for k in range(outer):

        @pl.when(a >= k)
        def _():
            for d in range(mid):
                arrive(name(a - k, lax.rem(y + d, mid), 1 - c))

            @pl.when(a + 1 < outer)
            def _():
                up(k).wait_send()

            for d in range(1, mid):
                side(k, d).wait_send()
            for d in range(mid):
                across(k, d).wait_send()


def gather(main_keys, index_keys):
    count = lax.axis_size("ctx")
    outer, mid = layout(count)
    channels = main_keys.shape[0] + index_keys.shape[0]
    return pl.pallas_call(
        functools.partial(gather_kernel, count),
        out_shape=jax.ShapeDtypeStruct((count, channels, main_keys.shape[1]), jnp.bfloat16),
        in_specs=[pl.BlockSpec(memory_space=pl.ANY)] * 2,
        out_specs=pl.BlockSpec(memory_space=pl.ANY),
        scratch_shapes=[
            pltpu.SemaphoreType.DMA((2,)),
            pltpu.SemaphoreType.DMA((count,)),
            pltpu.SemaphoreType.DMA((outer,)),
            pltpu.SemaphoreType.DMA((outer * max(mid - 1, 1),)),
            pltpu.SemaphoreType.DMA((outer * mid,)),
        ],
        compiler_params=pltpu.CompilerParams(collective_id=0, has_side_effects=True),
    )(main_keys, index_keys)


def scatter_kernel(count, terms, out, buf1, sum1, buf2, sum2, buf3, s1, r1, s2, r2, s3, r3):
    outer, mid = layout(count)
    a, y, c = position(mid)
    others = max(mid - 1, 1)

    def name(level, row, core):
        return (level * mid + row) * 2 + core

    greet(
        [name(lax.rem(a + d, outer), y, c) for d in range(1, outer)]
        + [name(a, lax.rem(y + d, mid), c) for d in range(1, mid)]
        + [name(a, y, 1 - c)]
    )

    def send(src, dst, send_sem, recv_sem, peer):
        return pltpu.make_async_remote_copy(
            src_ref=src,
            dst_ref=dst,
            send_sem=send_sem,
            recv_sem=recv_sem,
            device_id={"ctx": peer},
            device_id_type=mesh_ids,
        )

    def across(k):
        return send(terms.at[1 - c, k], buf1.at[k], s1.at[k], r1.at[k], name(a, y, 1 - c))

    def side(k, d):
        row = lax.rem(y + d, mid)
        spot = k * others + d - 1
        return send(sum1.at[k, row], buf2.at[spot], s2.at[spot], r2.at[spot], name(a, row, c))

    def down(k):
        spot = a - k - 1
        return send(sum2.at[k], buf3.at[spot], s3.at[k], r3.at[spot], name(k, y, c))

    for k in range(outer):

        @pl.when(a >= k)
        def _():
            across(k).start()

    for k in range(outer):

        @pl.when(a >= k)
        def _():
            across(k).wait_recv()
            sum1[k] = terms[c, k] + buf1[k]
            for d in range(1, mid):
                side(k, d).start()

    for k in range(outer):

        @pl.when(a >= k)
        def _():
            total = sum1[k, y]
            for d in range(1, mid):
                side(k, d).wait_recv()
                total = total + buf2[k * others + d - 1]
            sum2[k] = total

            @pl.when(a > k)
            def _():
                down(k).start()

            @pl.when(a == k)
            def _():
                out[...] = total

    for d in range(outer - 1):

        @pl.when(a + d + 1 < outer)
        def _():
            send(sum2.at[0], buf3.at[d], s3.at[0], r3.at[d], name(a, y, 1 - c)).wait_recv()
            out[...] += buf3[d]

    for k in range(outer):

        @pl.when(a >= k)
        def _():
            across(k).wait_send()
            for d in range(1, mid):
                side(k, d).wait_send()

            @pl.when(a > k)
            def _():
                down(k).wait_send()


def scatter(terms):
    count = lax.axis_size("ctx")
    outer, mid = layout(count)
    others = max(mid - 1, 1)
    tile = terms.shape[3:]
    return pl.pallas_call(
        functools.partial(scatter_kernel, count),
        out_shape=jax.ShapeDtypeStruct(tile, jnp.float32),
        in_specs=[pl.BlockSpec(memory_space=pltpu.VMEM)],
        out_specs=pl.BlockSpec(memory_space=pltpu.VMEM),
        scratch_shapes=[
            pltpu.VMEM((outer, mid) + tile, jnp.float32),
            pltpu.VMEM((outer, mid) + tile, jnp.float32),
            pltpu.VMEM((outer * others,) + tile, jnp.float32),
            pltpu.VMEM((outer,) + tile, jnp.float32),
            pltpu.VMEM((outer - 1,) + tile, jnp.float32),
            pltpu.SemaphoreType.DMA((outer,)),
            pltpu.SemaphoreType.DMA((outer,)),
            pltpu.SemaphoreType.DMA((outer * others,)),
            pltpu.SemaphoreType.DMA((outer * others,)),
            pltpu.SemaphoreType.DMA((outer,)),
            pltpu.SemaphoreType.DMA((outer - 1,)),
        ],
        compiler_params=pltpu.CompilerParams(
            collective_id=1, has_side_effects=True, vmem_limit_bytes=48 * 1024 * 1024
        ),
    )(terms)


def shards(main_queries, main_keys, index_queries, index_keys, head_weights, block_picks):
    tok = main_queries.shape[2]
    picks = block_picks
    count = lax.axis_size("ctx")
    keys = gather(main_keys, index_keys)
    row_loss, weight_grad, placed = compute(
        picks, main_queries, index_queries, head_weights, keys
    )
    outer, mid = layout(count)
    terms = placed.reshape((2, outer, mid) + placed.shape[1:])
    key_grad = scatter(terms)
    return (row_loss.reshape(tok), weight_grad, key_grad)


def solution(mesh):
    in_specs = (
        P(None, None, ("groups", "ctx")),
        P(None, ("groups", "ctx")),
        P(None, None, ("groups", "ctx")),
        P(None, ("groups", "ctx")),
        P(None, ("groups", "ctx")),
        P(("groups", "ctx"), None),
    )
    out_specs = (P(("groups", "ctx")), P(None, ("groups", "ctx")), P(None, ("groups", "ctx")))
    return jax.shard_map(shards, mesh=mesh, in_specs=in_specs, out_specs=out_specs, check_vma=False)
```

```python
import functools

import jax
import jax.numpy as jnp
from jax import lax
from jax.experimental import pallas as pl
from jax.experimental.pallas import tpu as pltpu
from jax.sharding import PartitionSpec as P

main_scale = 0.07216878364870322
index_scale = 0.08838834764831845
masked_value = -1e30
log2e = 1.4426950408889634


def compute_kernel(
    picks, mq, iq, hw, k0, k1, k2, k3, loss_ref, wg_ref, slot_ref, km, ki, eye, acc, raw, kt, gr, wf
):
    step = pl.program_id(0)
    steps = pl.num_programs(0)
    tok = mq.shape[2]
    latent = mq.shape[1]
    heads = mq.shape[0]
    slots = 4
    width = slots * tok

    @pl.when(step == 0)
    def _():
        rows = lax.broadcasted_iota(jnp.int32, (tok, tok), 0)
        cols = lax.broadcasted_iota(jnp.int32, (tok, tok), 1)
        diag = jnp.where(rows == cols, 1.0, 0.0).astype(jnp.bfloat16)
        eye[:, :tok] = diag
        eye[:, tok:] = diag
        for slot, key in enumerate((k0, k1, k2, k3)):
            here = pl.ds(slot * tok, tok)
            km[here, :latent] = key[0, :latent, :].T
            ki[here, :] = key[0, latent:, :].T
            if slot == 0:
                bias = jnp.where(rows > cols, masked_value, 0.0)
            else:
                bias = jnp.full((tok, tok), jnp.where(picks[0, slot] >= 0, 0.0, masked_value))
            km[here, latent:] = bias.astype(jnp.bfloat16)
        wf[...] = hw[...].astype(jnp.float32)
        acc[...] = jnp.zeros_like(acc)
        raw[...] = jnp.zeros_like(raw)
        slot_ref[...] = jnp.zeros_like(slot_ref)

    scale2 = main_scale * log2e

    def main_pair(i, _):
        h = 2 * i
        pair = jnp.concatenate([mq[h], mq[h + 1]], axis=1)
        query = jnp.concatenate([pair, eye[...]], axis=0)
        s = jnp.dot(km[...], query, preferred_element_type=jnp.float32)
        m = jnp.max(s, axis=0, keepdims=True)
        p = jnp.exp2((s - m) * scale2)
        p = p * (1.0 / jnp.sum(p, axis=0, keepdims=True))
        acc[...] += p[:, :tok] + p[:, tok:]
        j = step * heads + h
        ipair = jnp.concatenate([iq[j], iq[j + 1]], axis=1)
        before = jnp.dot(ki[...], ipair, preferred_element_type=jnp.float32)
        w = jnp.concatenate(
            [wf[pl.ds(j, 1), :], wf[pl.ds(j + 1, 1), :]], axis=1
        )
        a = jnp.maximum(before, 0.0) * w
        raw[...] += a[:, :tok] + a[:, tok:]
        return 0

    lax.fori_loop(0, heads // 2, main_pair, 0, unroll=4)

    @pl.when(step == steps - 1)
    def _():
        total_heads = heads * steps
        index_heads = iq.shape[0]
        target = acc[...] * (1.0 / total_heads)
        bias = km[:, latent:].astype(jnp.float32)
        logits = jnp.where(bias < 0.0, masked_value, raw[...] * index_scale)
        highest = jnp.max(logits, axis=0, keepdims=True)
        shifted = logits - highest
        powers = jnp.exp(shifted)
        denom = jnp.sum(powers, axis=0, keepdims=True)
        loss_ref[...] = -jnp.sum(target * (shifted - jnp.log(denom)), axis=0, keepdims=True)
        grad = powers / denom - target
        gr[:, :tok] = grad
        gr[:, tok:] = grad
        kt[...] = jnp.zeros_like(kt)

        def back_pair(i, _):
            j = 2 * i
            ipair = jnp.concatenate([iq[j], iq[j + 1]], axis=1)
            before = jnp.dot(ki[...], ipair, preferred_element_type=jnp.float32)
            g = gr[...]
            w = jnp.concatenate(
                [wf[pl.ds(j, 1), :], wf[pl.ds(j + 1, 1), :]], axis=1
            )
            part = jnp.sum(g * jnp.maximum(before, 0.0), axis=0, keepdims=True) * index_scale
            wg_ref[pl.ds(j, 1), :] = part[:, :tok]
            wg_ref[pl.ds(j + 1, 1), :] = part[:, tok:]
            up = jnp.where(before > 0.0, g * w, 0.0).astype(jnp.bfloat16)
            kt[...] += lax.dot_general(
                up, ipair, (((1,), (1,)), ((), ())), preferred_element_type=jnp.float32
            )
            return 0

        lax.fori_loop(0, index_heads // 2, back_pair, 0, unroll=4)
        for slot in range(slots):
            part = (kt[pl.ds(slot * tok, tok), :] * index_scale).T
            owner = picks[0, slot]
            half = slot_ref.shape[0] // 2

            @pl.when(owner >= 0)
            def _():
                slot_ref[lax.rem(owner, 2) * half + owner // 2] = part


def compute(picks, mq, iq, hw, keys):
    heads, latent, tok = mq.shape
    index_heads, dim, _ = iq.shape
    channels = latent + dim
    group = 8
    count = keys.shape[0]
    width = 4 * tok

    def key_spec(slot):
        return pl.BlockSpec(
            (1, channels, tok), lambda g, p: (jnp.maximum(p[0, slot], 0), 0, 0)
        )

    spec = pltpu.PrefetchScalarGridSpec(
        num_scalar_prefetch=1,
        grid=(heads // group,),
        in_specs=[
            pl.BlockSpec((group, latent, tok), lambda g, p: (g, 0, 0)),
            pl.BlockSpec((index_heads, dim, tok), lambda g, p: (0, 0, 0)),
            pl.BlockSpec((index_heads, tok), lambda g, p: (0, 0)),
        ]
        + [key_spec(slot) for slot in range(4)],
        out_specs=[
            pl.BlockSpec((1, tok), lambda g, p: (0, 0)),
            pl.BlockSpec((index_heads, tok), lambda g, p: (0, 0)),
            pl.BlockSpec((count, dim, tok), lambda g, p: (0, 0, 0)),
        ],
        scratch_shapes=[
            pltpu.VMEM((width, latent + tok), jnp.bfloat16),
            pltpu.VMEM((width, dim), jnp.bfloat16),
            pltpu.VMEM((tok, 2 * tok), jnp.bfloat16),
            pltpu.VMEM((width, tok), jnp.float32),
            pltpu.VMEM((width, tok), jnp.float32),
            pltpu.VMEM((width, dim), jnp.float32),
            pltpu.VMEM((width, 2 * tok), jnp.float32),
            pltpu.VMEM((index_heads, tok), jnp.float32),
        ],
    )
    return pl.pallas_call(
        compute_kernel,
        grid_spec=spec,
        out_shape=[
            jax.ShapeDtypeStruct((1, tok), jnp.float32),
            jax.ShapeDtypeStruct((index_heads, tok), jnp.float32),
            jax.ShapeDtypeStruct((count, dim, tok), jnp.float32),
        ],
        compiler_params=pltpu.CompilerParams(vmem_limit_bytes=48 * 1024 * 1024),
    )(picks, mq, iq, hw, keys, keys, keys, keys)


mesh_ids = pl.DeviceIdType.MESH


def layout(count):
    half = count // 2
    mid = 1
    while 4 * mid * mid <= half:
        mid *= 2
    return half // mid, mid


def position(mid):
    me = lax.axis_index("ctx")
    return me // (2 * mid), lax.rem(me // 2, mid), lax.rem(me, 2)


def greet(peers):
    barrier = pltpu.get_barrier_semaphore()
    for peer in peers:
        pl.semaphore_signal(barrier, inc=1, device_id={"ctx": peer}, device_id_type=mesh_ids)
    pl.semaphore_wait(barrier, len(peers))


def gather_kernel(count, main_ref, index_ref, out, local_sem, recv, zsend, ysend, csend):
    outer, mid = layout(count)
    a, y, c = position(mid)
    latent = main_ref.shape[0]
    channels = latent + index_ref.shape[0]

    def name(level, row, core):
        return (level * mid + row) * 2 + core

    me = name(a, y, c)
    own = [
        pltpu.make_async_copy(main_ref, out.at[me, pl.ds(0, latent)], local_sem.at[0]),
        pltpu.make_async_copy(
            index_ref, out.at[me, pl.ds(latent, channels - latent)], local_sem.at[1]
        ),
    ]
    for copy in own:
        copy.start()
    greet(
        [name(lax.rem(a + d, outer), y, c) for d in range(1, outer)]
        + [name(a, lax.rem(y + d, mid), c) for d in range(1, mid)]
        + [name(a, y, 1 - c)]
    )
    for copy in own:
        copy.wait()

    def send(block, peer, sem):
        return pltpu.make_async_remote_copy(
            src_ref=out.at[block],
            dst_ref=out.at[block],
            send_sem=sem,
            recv_sem=recv.at[block],
            device_id={"ctx": peer},
            device_id_type=mesh_ids,
        )

    def up(k):
        return send(name(a - k, y, c), name(a + 1, y, c), zsend.at[k])

    def side(k, d):
        return send(
            name(a - k, y, c), name(a, lax.rem(y + d, mid), c), ysend.at[k * max(mid - 1, 1) + d - 1]
        )

    def across(k, d):
        return send(
            name(a - k, lax.rem(y + d, mid), c), name(a, y, 1 - c), csend.at[k * mid + d]
        )

    def arrive(block):
        send(block, name(a, y, 1 - c), csend.at[0]).wait_recv()

    def first(k):
        @pl.when(a >= k)
        def _():
            if k > 0:
                arrive(name(a - k, y, c))

            @pl.when(a + 1 < outer)
            def _():
                up(k).start()

            for d in range(1, mid):
                side(k, d).start()
            across(k, 0).start()

    def second(k):
        @pl.when(a >= k)
        def _():
            for d in range(1, mid):
                arrive(name(a - k, lax.rem(y + d, mid), c))
                across(k, d).start()

    for k in range(outer):
        first(k)
        if k > 0:
            second(k - 1)
    second(outer - 1)
    for k in range(outer):

        @pl.when(a >= k)
        def _():
            for d in range(mid):
                arrive(name(a - k, lax.rem(y + d, mid), 1 - c))

            @pl.when(a + 1 < outer)
            def _():
                up(k).wait_send()

            for d in range(1, mid):
                side(k, d).wait_send()
            for d in range(mid):
                across(k, d).wait_send()


def gather(main_keys, index_keys):
    count = lax.axis_size("ctx")
    outer, mid = layout(count)
    channels = main_keys.shape[0] + index_keys.shape[0]
    return pl.pallas_call(
        functools.partial(gather_kernel, count),
        out_shape=jax.ShapeDtypeStruct((count, channels, main_keys.shape[1]), jnp.bfloat16),
        in_specs=[pl.BlockSpec(memory_space=pl.ANY)] * 2,
        out_specs=pl.BlockSpec(memory_space=pl.ANY),
        scratch_shapes=[
            pltpu.SemaphoreType.DMA((2,)),
            pltpu.SemaphoreType.DMA((count,)),
            pltpu.SemaphoreType.DMA((outer,)),
            pltpu.SemaphoreType.DMA((outer * max(mid - 1, 1),)),
            pltpu.SemaphoreType.DMA((outer * mid,)),
        ],
        compiler_params=pltpu.CompilerParams(collective_id=0, has_side_effects=True),
    )(main_keys, index_keys)


def scatter_kernel(count, terms, out, buf1, sum1, buf2, sum2, buf3, s1, r1, s2, r2, s3, r3):
    outer, mid = layout(count)
    a, y, c = position(mid)
    others = max(mid - 1, 1)

    def name(level, row, core):
        return (level * mid + row) * 2 + core

    greet(
        [name(lax.rem(a + d, outer), y, c) for d in range(1, outer)]
        + [name(a, lax.rem(y + d, mid), c) for d in range(1, mid)]
        + [name(a, y, 1 - c)]
    )

    def send(src, dst, send_sem, recv_sem, peer):
        return pltpu.make_async_remote_copy(
            src_ref=src,
            dst_ref=dst,
            send_sem=send_sem,
            recv_sem=recv_sem,
            device_id={"ctx": peer},
            device_id_type=mesh_ids,
        )

    def across(k):
        return send(terms.at[1 - c, k], buf1.at[k], s1.at[k], r1.at[k], name(a, y, 1 - c))

    def side(k, d):
        row = lax.rem(y + d, mid)
        spot = k * others + d - 1
        return send(sum1.at[k, row], buf2.at[spot], s2.at[spot], r2.at[spot], name(a, row, c))

    def down(k):
        spot = a - k - 1
        return send(sum2.at[k], buf3.at[spot], s3.at[k], r3.at[spot], name(k, y, c))

    for k in range(outer):

        @pl.when(a >= k)
        def _():
            across(k).start()

    for k in range(outer):

        @pl.when(a >= k)
        def _():
            across(k).wait_recv()
            sum1[k] = terms[c, k] + buf1[k]
            for d in range(1, mid):
                side(k, d).start()

    for k in range(outer):

        @pl.when(a >= k)
        def _():
            total = sum1[k, y]
            for d in range(1, mid):
                side(k, d).wait_recv()
                total = total + buf2[k * others + d - 1]
            sum2[k] = total

            @pl.when(a > k)
            def _():
                down(k).start()

            @pl.when(a == k)
            def _():
                out[...] = total

    for d in range(outer - 1):

        @pl.when(a + d + 1 < outer)
        def _():
            send(sum2.at[0], buf3.at[d], s3.at[0], r3.at[d], name(a, y, 1 - c)).wait_recv()
            out[...] += buf3[d]

    for k in range(outer):

        @pl.when(a >= k)
        def _():
            across(k).wait_send()
            for d in range(1, mid):
                side(k, d).wait_send()

            @pl.when(a > k)
            def _():
                down(k).wait_send()


def scatter(terms):
    count = lax.axis_size("ctx")
    outer, mid = layout(count)
    others = max(mid - 1, 1)
    tile = terms.shape[3:]
    return pl.pallas_call(
        functools.partial(scatter_kernel, count),
        out_shape=jax.ShapeDtypeStruct(tile, jnp.float32),
        in_specs=[pl.BlockSpec(memory_space=pltpu.VMEM)],
        out_specs=pl.BlockSpec(memory_space=pltpu.VMEM),
        scratch_shapes=[
            pltpu.VMEM((outer, mid) + tile, jnp.float32),
            pltpu.VMEM((outer, mid) + tile, jnp.float32),
            pltpu.VMEM((outer * others,) + tile, jnp.float32),
            pltpu.VMEM((outer,) + tile, jnp.float32),
            pltpu.VMEM((outer - 1,) + tile, jnp.float32),
            pltpu.SemaphoreType.DMA((outer,)),
            pltpu.SemaphoreType.DMA((outer,)),
            pltpu.SemaphoreType.DMA((outer * others,)),
            pltpu.SemaphoreType.DMA((outer * others,)),
            pltpu.SemaphoreType.DMA((outer,)),
            pltpu.SemaphoreType.DMA((outer - 1,)),
        ],
        compiler_params=pltpu.CompilerParams(
            collective_id=1, has_side_effects=True, vmem_limit_bytes=48 * 1024 * 1024
        ),
    )(terms)


def shards(main_queries, main_keys, index_queries, index_keys, head_weights, block_picks):
    tok = main_queries.shape[2]
    picks = block_picks
    count = lax.axis_size("ctx")
    keys = gather(main_keys, index_keys)
    row_loss, weight_grad, placed = compute(
        picks, main_queries, index_queries, head_weights, keys
    )
    outer, mid = layout(count)
    terms = placed.reshape((2, outer, mid) + placed.shape[1:])
    key_grad = scatter(terms)
    return (row_loss.reshape(tok), weight_grad, key_grad)


def solution(mesh):
    in_specs = (
        P(None, None, ("groups", "ctx")),
        P(None, ("groups", "ctx")),
        P(None, None, ("groups", "ctx")),
        P(None, ("groups", "ctx")),
        P(None, ("groups", "ctx")),
        P(("groups", "ctx"), None),
    )
    out_specs = (P(("groups", "ctx")), P(None, ("groups", "ctx")), P(None, ("groups", "ctx")))
    return jax.shard_map(shards, mesh=mesh, in_specs=in_specs, out_specs=out_specs, check_vma=False)
```
